256 devices in a mesh: shot: 64 (over z, x, core), blk: 4 (over y).
Axes of the slice: x: 4, y: 4, z: 8, core: 2. Of those that a mesh axis runs over, the one named last changes fastest.
Arguments:
- courant_sq: float32 [256, 96, 1024], P(('shot', 'blk')), may hold values from 0.05 to 0.25
- start_field: float32 [256, 96, 1024], P(('shot', 'blk')), may hold values from -6 to 6
- adjoint_state: float32 [256, 96, 1024], P(('shot', 'blk')), may hold values from -6 to 6
- observed: float32 [256, 16, 1024], P(('shot', 'blk')), may hold values from -6 to 6
- source_cell: int32 [256], replicated, may hold values from 0 to 32767
- lit_blocks: int32 [256, 8], P(('shot', 'blk')), may hold values from 0 to 1, as said below
- block_place: int32 [256], replicated, may hold values from 0 to 63, as said below
Outputs:
- gradient: float32 [256, 96, 128], P(('shot', 'blk'))
The draws below stay inside these ranges and needn't reach their ends.
Inputs may be any that keep to these rules, and one draw needn't show every extreme that they name: `lit_blocks`: each shot marks each block of its window 1 or 0; in every draw some 4 shots s * 4 + m, m = 0 .. 3, have every block marked 1. `block_place`: blocks k with the same k mod 4 carry distinct values.
All inputs are finite; a program needn't handle non-finite values.
Results may differ from the reference program's by a relative error of at most 0.0003.
Values sent between devices are 32-bit elements; how exact they have to be, the bound alone decides.
No kernel may reach another device: no remote copies, remote signals or barrier semaphores. Data moves between devices by JAX's collectives and lax.ppermute only.
A program may use at most 128 MiB of HBM per device.

```python
import jax
import jax.numpy as jnp
from jax import lax

NZ = 96
BW = 128
WIN = 8
STEPS = 16
SHOTS = 256
NB = 256
N_BLK = 4


def draw_lit_blocks(key, part):
    first_key, second_key = jax.random.split(jax.random.fold_in(key, 11))
    marked = (jax.random.randint(first_key, (SHOTS, WIN), 0, 4) > 0).astype(jnp.int32)
    full_group = jax.random.randint(second_key, (), 0, SHOTS // N_BLK)
    group_of_row = jnp.arange(SHOTS, dtype=jnp.int32) // N_BLK
    return jnp.where((group_of_row == full_group)[:, None], 1, marked).astype(jnp.int32)


def draw_block_place(key, part):
    column_keys = jax.random.split(jax.random.fold_in(key, 23), N_BLK)
    orders = jax.vmap(lambda column_key: jax.random.permutation(column_key, NB // N_BLK))(column_keys)
    return orders.T.reshape(NB).astype(jnp.int32)


def with_ends(drawn, own_key, least, top_value):
    spot = [jax.random.randint(jax.random.fold_in(own_key, axis), (), 0, length) for axis, length in enumerate(drawn.shape)]
    main_axis = drawn.shape.index(max(drawn.shape))
    next_to = spot[:main_axis] + [(spot[main_axis] + 1) % drawn.shape[main_axis]] + spot[main_axis + 1:]
    return drawn.at[tuple(spot)].set(least).at[tuple(next_to)].set(top_value)


def block_levels(rng, extent, cuts, smallest, top_value):
    level, own = 1.0, jax.random.fold_in(rng, 6)
    for dim, parts in cuts:
        draws = jnp.exp(jax.random.uniform(jax.random.fold_in(own, dim), (parts,), jnp.float32, smallest / len(cuts), top_value / len(cuts)))
        level = level * jnp.repeat(draws, extent[dim] // parts).reshape([-1 if axis == dim else 1 for axis in range(len(extent))])
    return level


def gaussian(own_key, shape, width, limit, cuts=(), kind=jnp.bfloat16):
    entries = jax.random.normal(own_key, shape, jnp.float32) * width
    if len(cuts) > 0:
        entries = block_levels(own_key, shape, cuts, -0.22, 0.18) * entries
    return jnp.clip(entries, min=-limit, max=limit).astype(kind)


def setup_inputs(seed: int = 0) -> dict:
    key_list = jax.random.split(jax.random.key(seed), 8)
    courant_sq = jnp.clip(0.05 + 0.2 * jax.random.uniform(key_list[0], (SHOTS, NZ, WIN * BW), jnp.float32) ** block_levels(key_list[0], (SHOTS, NZ, WIN * BW), ((0, 256),), -0.2, 0.2), 0.05, 0.25)
    start_field = gaussian(key_list[1], (SHOTS, NZ, WIN * BW), 1.0, 6.0, ((0, 256),), jnp.float32)
    adjoint_state = gaussian(key_list[2], (SHOTS, NZ, WIN * BW), 1.0, 6.0, ((0, 256),), jnp.float32)
    observed = gaussian(key_list[3], (SHOTS, STEPS, WIN * BW), 1.0, 6.0, ((0, 256),), jnp.float32)
    source_cell = with_ends(jax.random.randint(key_list[4], (SHOTS,), 0, NB * BW), jax.random.fold_in(key_list[4], 1), 0, (NB * BW) - 1).astype(jnp.int32)
    lit_blocks = draw_lit_blocks(jax.random.fold_in(key_list[7], 71), 0)
    block_place = draw_block_place(jax.random.fold_in(key_list[7], 71), 0)
    return dict(courant_sq=courant_sq, start_field=start_field, adjoint_state=adjoint_state, observed=observed, source_cell=source_cell, lit_blocks=lit_blocks, block_place=block_place)


stencil_weights = (-205.0 / 72.0, 8.0 / 5.0, -1.0 / 5.0, 8.0 / 315.0, -1.0 / 560.0)
receiver_row = 2
source_row = 6


def laplace(wavefield):
    depth_cells, lateral_cells = wavefield.shape
    padded = jnp.pad(wavefield, 4)
    result_sum = (2.0 * stencil_weights[0]) * wavefield
    for offset in range(1, 5):
        result_sum = result_sum + stencil_weights[offset] * (
            padded[4 + offset:4 + offset + depth_cells, 4:4 + lateral_cells]
            + padded[4 - offset:4 - offset + depth_cells, 4:4 + lateral_cells]
            + padded[4:4 + depth_cells, 4 + offset:4 + offset + lateral_cells]
            + padded[4:4 + depth_cells, 4 - offset:4 - offset + lateral_cells])
    return result_sum


def ricker(step_number):
    scaled_time = (step_number.astype(jnp.float32) - 4.0) * 0.55
    return 2.0 * (1.0 - 2.0 * scaled_time * scaled_time) * jnp.exp(-scaled_time * scaled_time)


def evolve(courant, initial, adjoint, observed, source_local):
    row_index = lax.broadcasted_iota(jnp.int32, courant.shape, 0)
    column_index = lax.broadcasted_iota(jnp.int32, courant.shape, 1)
    source_map = ((row_index == source_row) & (column_index == source_local)).astype(jnp.float32)
    receiver_mask = (row_index == receiver_row).astype(jnp.float32)

    def forward(state_pair, step_number):
        previous, current = state_pair
        following = 2.0 * current - previous + courant * (laplace(current) + ricker(step_number) * source_map)
        return (current, following), following

    _, advanced = lax.scan(forward, (initial, initial), jnp.arange(STEPS + 1, dtype=jnp.int32))
    fields = jnp.concatenate([initial[None], advanced], axis=0)
    predicted = fields[1:STEPS + 1, receiver_row, :]
    misfit = predicted - observed

    def backward(state_triple, inputs):
        newest, behind, imaging = state_triple
        residual_row, upper_field, middle_field, lower_field = inputs
        injected = receiver_mask * residual_row[None, :]
        refreshed = 2.0 * newest - behind + courant * (laplace(newest) + injected)
        imaging = imaging + refreshed * (upper_field - 2.0 * middle_field + lower_field)
        return (refreshed, newest, imaging), None

    begin = (adjoint, adjoint, jnp.zeros_like(adjoint))
    (_, _, imaging), _ = lax.scan(backward, begin, (misfit, fields[2:], fields[1:-1], fields[:-2]), reverse=True)
    return imaging * (-1.0 / STEPS)


def window_start(source_at, block_count):
    return jnp.clip(source_at // BW - WIN // 2, 0, block_count - WIN).astype(jnp.int32)


def reference(courant_sq, start_field, adjoint_state, observed, source_cell, lit_blocks, block_place):
    def one_shot(gradient_grid, inputs):
        courant, initial, adjoint, seen, source_at, lit_row = inputs
        first_block = window_start(source_at, NB)
        imaging = evolve(courant, initial, adjoint, seen, source_at - first_block * BW)
        blocks = imaging.reshape(NZ, WIN, BW).transpose(1, 0, 2) * lit_row.astype(jnp.float32)[:, None, None]
        anchor = jnp.int32(0)
        segment = lax.dynamic_slice(gradient_grid, (first_block, anchor, anchor), (WIN, NZ, BW))
        gradient_grid = lax.dynamic_update_slice(gradient_grid, segment + blocks, (first_block, anchor, anchor))
        return gradient_grid, None

    empty_grid = jnp.zeros((NB, NZ, BW), jnp.float32)
    gradient_grid, _ = lax.scan(one_shot, empty_grid, (courant_sq, start_field, adjoint_state, observed, source_cell, lit_blocks))
    block_order = jnp.arange(NB, dtype=jnp.int32)
    target_rows = block_place * N_BLK + block_order % N_BLK
    return jnp.zeros_like(gradient_grid).at[target_rows].set(gradient_grid)
```

```python
import jax
import jax.numpy as jnp
import numpy as np
from jax import lax
from jax.experimental import pallas as pl
from jax.experimental.pallas import tpu as pltpu
from jax.sharding import Mesh, PartitionSpec as P

NZ = 96
BW = 128
WIN = 8
STEPS = 16
NB = 256
N_Z, N_X, N_CORE, N_Y = 8, 4, 2, 4
AXES = ("z", "x", "core", "y")
F32 = jnp.float32
BF16 = jnp.bfloat16

CENTRE, TAPS, REST, SCALE = -28672.0, (8064.0, -1008.0, 128.0, -9.0), -28.0, 5040.0
receiver_row = 2
source_row = 6


def lateral_matrix():
    m = np.zeros((BW, 2 * BW), np.float32)
    for i in range(BW):
        for k in range(-4, 5):
            column = i + k
            weight = TAPS[abs(k) - 1] if k else CENTRE
            if 0 <= column < BW:
                m[i, column] = weight
            else:
                m[i, BW + column % BW] = weight
    return np.concatenate([m, m], 0)


def depth_matrix():
    m = np.zeros((NZ, NZ), np.float32)
    for i in range(NZ):
        for k in range(-4, 5):
            if 0 <= i + k < NZ:
                m[i, i + k] = TAPS[abs(k) - 1] if k else REST
    return np.concatenate([m, m], 1)


def halves(v):
    high = v.astype(BF16)
    return high, v - high.astype(F32)


def put_halves(x_ref, t, v):
    high, rest = halves(v)
    x_ref[t, :, 0:BW] = high
    x_ref[t, :, BW : 2 * BW] = rest.astype(BF16)


def laplace(x_ref, lateral, depth):
    sides = [jnp.dot(x_ref[t], lateral, preferred_element_type=F32) for t in range(WIN)]
    deep = []
    for p in range(0, WIN, 2):
        pair = [
            jnp.concatenate([x_ref[p][:, s : s + BW], x_ref[p + 1][:, s : s + BW]], 1)
            for s in (0, BW)
        ]
        deep.append(jnp.dot(depth, jnp.concatenate(pair, 0), preferred_element_type=F32))
    from_left = lax.broadcasted_iota(jnp.int32, (NZ, BW), 1) < BW // 2
    zeros = jnp.zeros((NZ, BW), F32)
    result = []
    for t in range(WIN):
        spilled = jnp.where(
            from_left,
            sides[t - 1][:, BW:] if t > 0 else zeros,
            sides[t + 1][:, BW:] if t < WIN - 1 else zeros,
        )
        result.append((sides[t][:, :BW] + deep[t // 2][:, t % 2 * BW : (t % 2 + 1) * BW]) + spilled)
    return result


def add_top(v, top):
    return jnp.concatenate([v[0:8] + top, v[8:]], 0)


def first_block(cell):
    return jnp.clip(lax.shift_right_logical(cell, 7) - WIN // 2, 0, NB - WIN)


def own_shot():
    z, x, core, y = (lax.axis_index(a) for a in AXES)
    return ((z * N_X + x) * N_CORE + core) * N_Y + y


def wave_kernel(
    cell_ref, lit_ref, ricker_ref, c_in, u_in, a_in, obs_ref, lateral_ref, depth_ref, out_ref,
    c_s, u_s, a_s, obs_s, lat_s, dep_s, q_s, v_s, g_s, hist_s, x_s, y_s, top_s, row_s, sem,
):
    copies = []
    for i, (src, dst) in enumerate(((u_in, u_s), (c_in, c_s), (a_in, a_s))):
        for t in range(WIN):
            copies.append(
                pltpu.make_async_copy(src.at[0, :, pl.ds(t * BW, BW)], dst.at[t], sem.at[i * WIN + t])
            )
    for i, (src, dst) in enumerate(((lateral_ref, lat_s), (depth_ref, dep_s), (obs_ref.at[0], obs_s))):
        copies.append(pltpu.make_async_copy(src, dst, sem.at[3 * WIN + i]))
    for copy in copies:
        copy.start()
    v_s[...] = jnp.zeros_like(v_s)
    cell = cell_ref[own_shot()]
    first = first_block(cell)
    source_column = cell - first * BW
    rows = lax.broadcasted_iota(jnp.int32, (8, BW), 0)
    columns = lax.broadcasted_iota(jnp.int32, (8, BW), 1)
    for copy in copies:
        copy.wait()
    lateral = lat_s[...]
    depth = dep_s[...]

    def whole_laplace(field):
        for t in range(WIN):
            high, rest = halves(field[t])
            low, last = halves(rest)
            x_s[t, :, 0:BW] = high
            x_s[t, :, BW : 2 * BW] = low
            put_halves(y_s, t, last)
        part = laplace(x_s, lateral, depth)
        for t in range(WIN):
            q_s[t] = part[t]
        part = laplace(y_s, lateral, depth)
        for t in range(WIN):
            q_s[t] = q_s[t] + part[t]

    def add_laplace():
        part = laplace(x_s, lateral, depth)
        for t in range(WIN):
            q_s[t] = q_s[t] + part[t]

    for t in range(WIN):
        c_s[t] = c_s[t] * (1.0 / SCALE)
        top_s[t] = u_s[t, 0:8]
    whole_laplace(u_s)

    def forward(n, carry):
        force = ricker_ref[n] * SCALE
        for t in range(WIN):
            at_source = (rows == source_row) & (columns + t * BW == source_column)
            v = v_s[t] + c_s[t] * add_top(q_s[t], jnp.where(at_source, force, 0.0))
            v_s[t] = v
            hist_s[n, t] = v
            top = top_s[t] + v[0:8]
            top_s[t] = top
            row_s[n, t] = top
            put_halves(x_s, t, v)
        add_laplace()
        return carry

    lax.fori_loop(0, STEPS + 1, forward, 0)
    for n in range(STEPS):
        for t in range(WIN):
            misfit = row_s[n, t] - obs_s[n : n + 1, t * BW : (t + 1) * BW]
            row_s[n, t] = jnp.where(rows == receiver_row, misfit, 0.0) * SCALE
    whole_laplace(a_s)
    for t in range(WIN):
        v_s[t] = jnp.zeros((NZ, BW), F32)
        g_s[t] = a_s[t] * (hist_s[STEPS, t] - hist_s[0, t])

    def backward(i, carry):
        n = STEPS - i
        for t in range(WIN):
            v = v_s[t] + c_s[t] * add_top(q_s[t], row_s[n - 1, t])
            v_s[t] = v
            g_s[t] = g_s[t] + v * (hist_s[n, t] - hist_s[0, t])
            put_halves(x_s, t, v)
        add_laplace()
        return carry

    lax.fori_loop(0, STEPS, backward, 0)
    for j in range(WIN):
        block = g_s[j] * (lit_ref[0, j].astype(F32) * (-1.0 / STEPS))
        owner = (first + j) & (N_Y - 1)
        for x in range(N_X):
            out_ref[x, owner, j // N_Y] = block


def route_kernel(cell_ref, place_ref, blocks_ref, own_ref, other_ref):
    z, x_own, core_own, y_own = (lax.axis_index(a) for a in AXES)
    own_ref[...] = jnp.zeros_like(own_ref)
    other_ref[...] = jnp.zeros_like(other_ref)

    def from_device(i, carry):
        x, y = lax.shift_right_logical(i, 2), i & (N_Y - 1)
        first = first_block(cell_ref[((z * N_X + x) * N_CORE + core_own) * N_Y + y])
        k = first + ((y_own - first) & (N_Y - 1))
        for h in range(WIN // N_Y):
            place = place_ref[k + N_Y * h]
            to_z = lax.shift_right_logical(place, 3)
            to_x = lax.shift_right_logical(place, 1) & (N_X - 1)
            to_core = place & (N_CORE - 1)

            @pl.when((to_x == x_own) & (to_core == core_own))
            def _():
                own_ref[to_z] = own_ref[to_z] + blocks_ref[x, y, h]

            @pl.when((to_x == x_own) & (to_core != core_own))
            def _():
                other_ref[to_z] = other_ref[to_z] + blocks_ref[x, y, h]

        return carry

    lax.fori_loop(0, N_X * N_Y, from_device, 0)


def ricker(step_number):
    scaled_time = (step_number.astype(F32) - 4.0) * 0.55
    return 2.0 * (1.0 - 2.0 * scaled_time * scaled_time) * jnp.exp(-scaled_time * scaled_time)


def local(courant_sq, start_field, adjoint_state, observed, source_cell, lit_blocks, block_place):
    smem = pl.BlockSpec(memory_space=pltpu.SMEM)
    vmem = pl.BlockSpec(memory_space=pltpu.VMEM)
    hbm = pl.BlockSpec(memory_space=pltpu.HBM)
    field = pltpu.VMEM((WIN, NZ, BW), F32)
    parts = pltpu.VMEM((WIN, NZ, 2 * BW), BF16)
    forces = ricker(jnp.arange(STEPS + 1, dtype=jnp.int32))
    pieces = pl.pallas_call(
        wave_kernel,
        out_shape=jax.ShapeDtypeStruct((N_X, N_Y, WIN // N_Y, NZ, BW), F32),
        in_specs=[smem] * 3 + [hbm] * 6,
        out_specs=vmem,
        scratch_shapes=[
            field, field, field,
            pltpu.VMEM((STEPS, WIN * BW), F32),
            pltpu.VMEM((2 * BW, 2 * BW), BF16),
            pltpu.VMEM((NZ, 2 * NZ), BF16),
            field, field, field,
            pltpu.VMEM((STEPS + 1, WIN, NZ, BW), F32),
            parts, parts,
            pltpu.VMEM((WIN, 8, BW), F32),
            pltpu.VMEM((STEPS + 1, WIN, 8, BW), F32),
            pltpu.SemaphoreType.DMA((3 * WIN + 3,)),
        ],
        compiler_params=pltpu.CompilerParams(vmem_limit_bytes=58 << 20),
        name="wave",
    )(
        source_cell, lit_blocks, forces, courant_sq, start_field, adjoint_state, observed,
        jnp.asarray(lateral_matrix(), BF16), jnp.asarray(depth_matrix(), BF16),
    )
    pieces = pieces.reshape(N_X * N_Y, WIN // N_Y, NZ, BW)
    pieces = lax.all_to_all(pieces, ("x", "y"), 0, 0, tiled=True)
    slots = jax.ShapeDtypeStruct((N_Z, NZ, BW), F32)
    own, other = pl.pallas_call(
        route_kernel,
        out_shape=(slots, slots),
        in_specs=[smem] * 2 + [vmem],
        out_specs=(vmem, vmem),
        compiler_params=pltpu.CompilerParams(vmem_limit_bytes=16 << 20),
        name="route",
    )(source_cell, block_place, pieces.reshape(N_X, N_Y, WIN // N_Y, NZ, BW))
    own = own + lax.ppermute(other, "core", [(0, 1), (1, 0)])
    return jnp.sum(lax.all_to_all(own, "z", 0, 0, tiled=True), axis=0, keepdims=True)


def solution(mesh):
    split_mesh = Mesh(mesh.devices.reshape(N_Z, N_X, N_CORE, N_Y), AXES)
    split = P(AXES, None, None)
    return jax.shard_map(
        local,
        mesh=split_mesh,
        in_specs=(split, split, split, split, P(), P(AXES, None), P()),
        out_specs=split,
        check_vma=False,
    )
```

```python
import jax
import jax.numpy as jnp
import numpy as np
from jax import lax
from jax.experimental import pallas as pl
from jax.experimental.pallas import tpu as pltpu
from jax.sharding import Mesh, PartitionSpec as P

NZ = 96
BW = 128
WIN = 8
STEPS = 16
NB = 256
N_Z, N_X, N_CORE, N_Y = 8, 4, 2, 4
AXES = ("z", "x", "core", "y")
F32 = jnp.float32
BF16 = jnp.bfloat16

CENTRE, TAPS, REST, SCALE = -28672.0, (8064.0, -1008.0, 128.0, -9.0), -28.0, 5040.0
Z_GROUPS = ((0,), (1, 4, -2), (-1, 2), (3,), (-3,))
receiver_row = 2
source_row = 6


def lateral_matrix():
    m = np.zeros((BW, 2 * BW), np.float32)
    for i in range(BW):
        for k in range(-4, 5):
            column = i + k
            weight = TAPS[abs(k) - 1] if k else CENTRE
            if 0 <= column < BW:
                m[i, column] = weight
            else:
                m[i, BW + column % BW] = weight
    return np.concatenate([m, m], 0)


def depth_matrix():
    m = np.zeros((NZ, NZ), np.float32)
    for i in range(NZ):
        for k in range(-4, 5):
            if 0 <= i + k < NZ:
                m[i, i + k] = TAPS[abs(k) - 1] if k else REST
    return np.concatenate([m, m], 1)


def halves(v):
    high = v.astype(BF16)
    return high, v - high.astype(F32)


def put_halves(x_ref, t, v):
    high, rest = halves(v)
    x_ref[t, :, 0:BW] = high
    x_ref[t, :, BW : 2 * BW] = rest.astype(BF16)


def laplace(x_ref, lateral, depth):
    sides = [jnp.dot(x_ref[t], lateral, preferred_element_type=F32) for t in range(WIN)]
    deep = []
    for p in range(0, WIN, 2):
        pair = [
            jnp.concatenate([x_ref[p][:, s : s + BW], x_ref[p + 1][:, s : s + BW]], 1)
            for s in (0, BW)
        ]
        deep.append(jnp.dot(depth, jnp.concatenate(pair, 0), preferred_element_type=F32))
    from_left = lax.broadcasted_iota(jnp.int32, (NZ, BW), 1) < BW // 2
    zeros = jnp.zeros((NZ, BW), F32)
    result = []
    for t in range(WIN):
        spilled = jnp.where(
            from_left,
            sides[t - 1][:, BW:] if t > 0 else zeros,
            sides[t + 1][:, BW:] if t < WIN - 1 else zeros,
        )
        result.append((sides[t][:, :BW] + deep[t // 2][:, t % 2 * BW : (t % 2 + 1) * BW]) + spilled)
    return result


def add_top(v, top):
    return jnp.concatenate([v[0:8] + top, v[8:]], 0)


def first_block(cell):
    return jnp.clip(lax.shift_right_logical(cell, 7) - WIN // 2, 0, NB - WIN)


def own_shot():
    z, x, core, y = (lax.axis_index(a) for a in AXES)
    return ((z * N_X + x) * N_CORE + core) * N_Y + y


def wave_kernel(
    cell_ref, lit_ref, c_in, u_in, a_in, obs_ref, lateral_ref, depth_ref, *refs
):
    out_refs = refs[:N_Y]
    (c_s, u_s, a_s, obs_s, lat_s, dep_s, q_s, v_s, g_s, hist_s, x_s, y_s, top_s, row_s, sem) = refs[N_Y:]
    copies = []
    for i, (src, dst) in enumerate(((u_in, u_s), (c_in, c_s), (a_in, a_s))):
        for t in range(WIN):
            copies.append(
                pltpu.make_async_copy(src.at[0, :, pl.ds(t * BW, BW)], dst.at[t], sem.at[i * WIN + t])
            )
    for i, (src, dst) in enumerate(((lateral_ref, lat_s), (depth_ref, dep_s), (obs_ref.at[0], obs_s))):
        copies.append(pltpu.make_async_copy(src, dst, sem.at[3 * WIN + i]))
    for copy in copies:
        copy.start()
    v_s[...] = jnp.zeros_like(v_s)
    cell = cell_ref[own_shot()]
    first = first_block(cell)
    source_column = cell - first * BW
    rows = lax.broadcasted_iota(jnp.int32, (8, BW), 0)
    columns = lax.broadcasted_iota(jnp.int32, (8, BW), 1)
    for copy in copies:
        copy.wait()
    lateral = lat_s[...]
    depth = dep_s[...]

    def whole_laplace(field):
        for t in range(WIN):
            high, rest = halves(field[t])
            low, last = halves(rest)
            x_s[t, :, 0:BW] = high
            x_s[t, :, BW : 2 * BW] = low
            put_halves(y_s, t, last)
        part = laplace(x_s, lateral, depth)
        for t in range(WIN):
            q_s[t] = part[t]
        part = laplace(y_s, lateral, depth)
        for t in range(WIN):
            q_s[t] = q_s[t] + part[t]

    def add_laplace():
        part = laplace(x_s, lateral, depth)
        for t in range(WIN):
            q_s[t] = q_s[t] + part[t]

    for t in range(WIN):
        c_s[t] = c_s[t] * (1.0 / SCALE)
        top_s[t] = u_s[t, 0:8]
    whole_laplace(u_s)

    def forward(n, carry):
        force = ricker(jnp.full((8, BW), n, jnp.int32)) * SCALE
        for t in range(WIN):
            at_source = (rows == source_row) & (columns + t * BW == source_column)
            v = v_s[t] + c_s[t] * add_top(q_s[t], jnp.where(at_source, force, 0.0))
            v_s[t] = v
            hist_s[n, t] = v
            top = top_s[t] + v[0:8]
            top_s[t] = top
            row_s[n, t] = top
            put_halves(x_s, t, v)
        add_laplace()
        return carry

    lax.fori_loop(0, STEPS + 1, forward, 0)
    for n in range(STEPS):
        for t in range(WIN):
            misfit = row_s[n, t] - obs_s[n : n + 1, t * BW : (t + 1) * BW]
            row_s[n, t] = jnp.where(rows == receiver_row, misfit, 0.0) * SCALE
    whole_laplace(a_s)
    for t in range(WIN):
        v_s[t] = jnp.zeros((NZ, BW), F32)
        g_s[t] = a_s[t] * (hist_s[STEPS, t] - hist_s[0, t])

    def backward(i, carry):
        n = STEPS - i
        for t in range(WIN):
            v = v_s[t] + c_s[t] * add_top(q_s[t], row_s[n - 1, t])
            v_s[t] = v
            g_s[t] = g_s[t] + v * (hist_s[n, t] - hist_s[0, t])
            put_halves(x_s, t, v)
        add_laplace()
        return carry

    lax.fori_loop(0, STEPS, backward, 0)
    y = lax.axis_index("y")
    for d, out_ref in enumerate(out_refs):
        for h in range(WIN // N_Y):
            j = ((y + d - first) & (N_Y - 1)) + N_Y * h
            out_ref[h] = g_s[j] * (lit_ref[0, j].astype(F32) * (-1.0 / STEPS))


def route_kernel(cell_ref, place_ref, *refs):
    gathered, (own_ref, other_ref) = refs[:-2], refs[-2:]
    z, x_own, core_own, y_own = (lax.axis_index(a) for a in AXES)
    own_ref[...] = jnp.zeros_like(own_ref)
    other_ref[...] = jnp.zeros_like(other_ref)
    for i, blocks_ref in enumerate(gathered):
        x = (x_own + (0, -1, 1, 2)[i // 2]) & (N_X - 1)
        for d in range(2):
            y = (y_own - (2 * (i % 2) + d)) & (N_Y - 1)
            first = first_block(cell_ref[((z * N_X + x) * N_CORE + core_own) * N_Y + y])
            k = first + ((y_own - first) & (N_Y - 1))
            for h in range(WIN // N_Y):
                place = place_ref[k + N_Y * h]
                slot = (lax.shift_right_logical(place, 3) - z) & (N_Z - 1)
                to_x = lax.shift_right_logical(place, 1) & (N_X - 1)
                to_core = place & (N_CORE - 1)

                @pl.when((to_x == x_own) & (to_core == core_own))
                def _():
                    own_ref[slot] = own_ref[slot] + blocks_ref[2 * d + h]

                @pl.when((to_x == x_own) & (to_core != core_own))
                def _():
                    other_ref[slot] = other_ref[slot] + blocks_ref[2 * d + h]


def join_kernel(own_ref, other_ref, *out_refs):
    for offsets, out_ref in zip(Z_GROUPS, out_refs, strict=True):
        for i, d in enumerate(offsets):
            out_ref[i] = own_ref[d % N_Z] + other_ref[d % N_Z]


def shift(v, axis, size, by):
    return lax.ppermute(v, axis, [(i, (i + by) % size) for i in range(size)])


def ricker(step_number):
    scaled_time = (step_number.astype(F32) - 4.0) * 0.55
    return 2.0 * (1.0 - 2.0 * scaled_time * scaled_time) * jnp.exp(-scaled_time * scaled_time)


def local(courant_sq, start_field, adjoint_state, observed, source_cell, lit_blocks, block_place):
    smem = pl.BlockSpec(memory_space=pltpu.SMEM)
    vmem = pl.BlockSpec(memory_space=pltpu.VMEM)
    hbm = pl.BlockSpec(memory_space=pltpu.HBM)
    field = pltpu.VMEM((WIN, NZ, BW), F32)
    parts = pltpu.VMEM((WIN, NZ, 2 * BW), BF16)
    piece = jax.ShapeDtypeStruct((WIN // N_Y, NZ, BW), F32)
    pieces = pl.pallas_call(
        wave_kernel,
        out_shape=(piece,) * N_Y,
        in_specs=[smem] * 2 + [hbm] * 6,
        out_specs=(vmem,) * N_Y,
        scratch_shapes=[
            field, field, field,
            pltpu.VMEM((STEPS, WIN * BW), F32),
            pltpu.VMEM((2 * BW, 2 * BW), BF16),
            pltpu.VMEM((NZ, 2 * NZ), BF16),
            field, field, field,
            pltpu.VMEM((STEPS + 1, WIN, NZ, BW), F32),
            parts, parts,
            pltpu.VMEM((WIN, 8, BW), F32),
            pltpu.VMEM((STEPS + 1, WIN, 8, BW), F32),
            pltpu.SemaphoreType.DMA((3 * WIN + 3,)),
        ],
        compiler_params=pltpu.CompilerParams(vmem_limit_bytes=58 << 20),
        name="wave",
    )(
        source_cell, lit_blocks, courant_sq, start_field, adjoint_state, observed,
        jnp.asarray(lateral_matrix(), BF16), jnp.asarray(depth_matrix(), BF16),
    )
    near = jnp.concatenate([pieces[0], shift(pieces[1], "y", N_Y, 1)], 0)
    far = jnp.concatenate([shift(pieces[2], "y", N_Y, 2), shift(pieces[3], "y", N_Y, 3)], 0)
    near_left, near_right = shift(near, "x", N_X, 1), shift(near, "x", N_X, -1)
    far_left, far_right = shift(far, "x", N_X, 1), shift(far, "x", N_X, -1)
    gathered = (
        near, far, near_left, far_left, near_right, far_right,
        shift(near_left, "x", N_X, 1), shift(far_right, "x", N_X, -1),
    )
    slots = jax.ShapeDtypeStruct((N_Z, NZ, BW), F32)
    own, other = pl.pallas_call(
        route_kernel,
        out_shape=(slots, slots),
        in_specs=[smem] * 2 + [vmem] * len(gathered),
        out_specs=(vmem, vmem),
        compiler_params=pltpu.CompilerParams(vmem_limit_bytes=16 << 20),
        name="route",
    )(source_cell, block_place, *gathered)
    here, up, down, up_three, down_three = pl.pallas_call(
        join_kernel,
        out_shape=tuple(jax.ShapeDtypeStruct((len(g), NZ, BW), F32) for g in Z_GROUPS),
        in_specs=[vmem, vmem],
        out_specs=(vmem,) * len(Z_GROUPS),
        compiler_params=pltpu.CompilerParams(vmem_limit_bytes=16 << 20),
        name="join",
    )(own, shift(other, "core", N_CORE, 1))
    up, down = shift(up, "z", N_Z, 1), shift(down, "z", N_Z, -1)
    up_three = shift(up_three + up[1:2] + down[1:], "z", N_Z, 3)
    down_three = shift(down_three + up[2:], "z", N_Z, -3)
    return (here + up[:1] + down[:1]) + (up_three + down_three)


def solution(mesh):
    split_mesh = Mesh(mesh.devices.reshape(N_Z, N_X, N_CORE, N_Y), AXES)
    split = P(AXES, None, None)
    return jax.shard_map(
        local,
        mesh=split_mesh,
        in_specs=(split, split, split, split, P(), P(AXES, None), P()),
        out_specs=split,
        check_vma=False,
    )
```

```python
import jax
import jax.numpy as jnp
import numpy as np
from jax import lax
from jax.experimental import pallas as pl
from jax.experimental.pallas import tpu as pltpu
from jax.sharding import Mesh, PartitionSpec as P

NZ = 96
BW = 128
WIN = 8
STEPS = 16
NB = 256
N_Z, N_X, N_CORE, N_Y = 8, 4, 2, 4
AXES = ("z", "x", "core", "y")
F32 = jnp.float32
BF16 = jnp.bfloat16

CENTRE, TAPS, REST, SCALE = -28672.0, (8064.0, -1008.0, 128.0, -9.0), -28.0, 5040.0
X_STEPS = (0, 1, -1, 2)
Z_GROUPS = ((0,), (1, 4, -2), (-1, 2), (3,), (-3,))
receiver_row = 2
source_row = 6


def lateral_matrix():
    m = np.zeros((BW, 2 * BW), np.float32)
    for i in range(BW):
        for k in range(-4, 5):
            column = i + k
            weight = TAPS[abs(k) - 1] if k else CENTRE
            if 0 <= column < BW:
                m[i, column] = weight
            else:
                m[i, BW + column % BW] = weight
    return np.concatenate([m, m], 0)


def depth_matrix():
    m = np.zeros((NZ, NZ), np.float32)
    for i in range(NZ):
        for k in range(-4, 5):
            if 0 <= i + k < NZ:
                m[i, i + k] = TAPS[abs(k) - 1] if k else REST
    return np.concatenate([m, m], 1)


def halves(v):
    high = v.astype(BF16)
    return high, v - high.astype(F32)


def block(t):
    return slice(t * BW, (t + 1) * BW)


def put_halves(x_ref, t, v):
    high, rest = halves(v)
    x_ref[t, :, 0:BW] = high
    x_ref[t, :, BW : 2 * BW] = rest.astype(BF16)


def laplace(x_ref, lateral, depth):
    halves_of_all = x_ref[...].reshape(WIN * NZ, 2 * BW)
    sides = jnp.dot(halves_of_all, lateral, preferred_element_type=F32).reshape(WIN, NZ, 2 * BW)
    deep = []
    for p in range(0, WIN, 2):
        pair = [
            jnp.concatenate([x_ref[p][:, s : s + BW], x_ref[p + 1][:, s : s + BW]], 1)
            for s in (0, BW)
        ]
        deep.append(jnp.dot(depth, jnp.concatenate(pair, 0), preferred_element_type=F32))
    from_left = lax.broadcasted_iota(jnp.int32, (NZ, BW), 1) < BW // 2
    zeros = jnp.zeros((NZ, BW), F32)
    result = []
    for t in range(WIN):
        spilled = jnp.where(
            from_left,
            sides[t - 1][:, BW:] if t > 0 else zeros,
            sides[t + 1][:, BW:] if t < WIN - 1 else zeros,
        )
        result.append((sides[t][:, :BW] + deep[t // 2][:, t % 2 * BW : (t % 2 + 1) * BW]) + spilled)
    return result


def add_top(v, top):
    return jnp.concatenate([v[0:8] + top, v[8:]], 0)


def first_block(cell):
    return jnp.clip(lax.shift_right_logical(cell, 7) - WIN // 2, 0, NB - WIN)


def own_shot():
    z, x, core, y = (lax.axis_index(a) for a in AXES)
    return ((z * N_X + x) * N_CORE + core) * N_Y + y


def wave_kernel(
    cell_in, lit_in, c_in, u_in, a_in, obs_ref, lateral_ref, depth_ref, *refs
):
    out_refs = refs[:N_Y]
    (c_s, u_s, a_s, obs_s, lat_s, dep_s, q_s, v_s, g_s, hist_s, x_s, y_s, top_s, row_s, cell_ref, lit_ref, sem) = refs[N_Y:]
    copies = [
        pltpu.make_async_copy(src, dst, sem.at[i])
        for i, (src, dst) in enumerate(
            (
                (u_in.at[0], u_s), (lateral_ref, lat_s), (depth_ref, dep_s), (cell_in, cell_ref),
                (c_in.at[0], c_s), (a_in.at[0], a_s), (obs_ref.at[0], obs_s), (lit_in, lit_ref),
            )
        )
    ]
    for copy in copies:
        copy.start()
    for copy in copies[:4]:
        copy.wait()
    cell = cell_ref[own_shot()]
    first = first_block(cell)
    source_column = cell - first * BW
    rows = lax.broadcasted_iota(jnp.int32, (8, BW), 0)
    columns = lax.broadcasted_iota(jnp.int32, (8, BW), 1)
    lateral = lat_s[...]
    depth = dep_s[...]

    def whole_laplace(field):
        for t in range(WIN):
            high, rest = halves(field[:, block(t)])
            low, last = halves(rest)
            x_s[t, :, 0:BW] = high
            x_s[t, :, BW : 2 * BW] = low
            put_halves(y_s, t, last)
        first_parts, last_parts = laplace(x_s, lateral, depth), laplace(y_s, lateral, depth)
        return [p + q for p, q in zip(first_parts, last_parts, strict=True)]

    def source(n, t):
        at_source = (rows == source_row) & (columns + t * BW == source_column)
        return jnp.where(at_source, ricker(jnp.full((8, BW), n, jnp.int32)) * SCALE, 0.0)

    def keep_top(n, t, v):
        top = top_s[t] + v[0:8]
        top_s[t] = top
        row_s[n, t] = top

    part = whole_laplace(u_s)
    copies[4].wait()
    for t in range(WIN):
        c = c_s[:, block(t)] * (1.0 / SCALE)
        c_s[:, block(t)] = c
        q_s[t] = part[t]
        v = c * add_top(part[t], source(0, t))
        hist_s[0, t] = v
        top_s[t] = u_s[0:8, block(t)]
        keep_top(0, t, v)
        put_halves(x_s, t, v)

    def forward(n, x_ref, next_ref):
        part = laplace(x_ref, lateral, depth)
        for t in range(WIN):
            q = q_s[t] + part[t]
            q_s[t] = q
            v = hist_s[n - 1, t] + c_s[:, block(t)] * add_top(q, source(n, t))
            hist_s[n, t] = v
            keep_top(n, t, v)
            put_halves(next_ref, t, v)

    def forward_pair(i, carry):
        forward(2 * i + 1, x_s, y_s)
        forward(2 * i + 2, y_s, x_s)
        return carry

    lax.fori_loop(0, STEPS // 2, forward_pair, 0, unroll=4)
    for copy in copies[5:]:
        copy.wait()
    for n in range(STEPS):
        for t in range(WIN):
            misfit = row_s[n, t] - obs_s[n : n + 1, block(t)]
            row_s[n, t] = jnp.where(rows == receiver_row, misfit, 0.0) * SCALE
    part = whole_laplace(a_s)
    for t in range(WIN):
        q_s[t] = part[t]
        w = c_s[:, block(t)] * add_top(part[t], row_s[STEPS - 1, t])
        v_s[t] = w
        g_s[t] = (a_s[:, block(t)] + w) * (hist_s[STEPS, t] - hist_s[0, t])
        put_halves(x_s, t, w)

    def backward(n, x_ref, next_ref, image):
        part = laplace(x_ref, lateral, depth)
        for t in range(WIN):
            q = q_s[t] + part[t]
            q_s[t] = q
            before = v_s[t]
            w = before + c_s[:, block(t)] * add_top(q, row_s[n - 1, t])
            v_s[t] = w
            if image == 1:
                g_s[t] = g_s[t] + w * (hist_s[n, t] - hist_s[0, t])
            if image == 2:
                later = before * (hist_s[n + 1, t] - hist_s[0, t])
                g_s[t] = g_s[t] + (w * (hist_s[n, t] - hist_s[0, t]) + later)
            if next_ref is not None:
                put_halves(next_ref, t, w)

    def backward_pair(i, carry):
        backward(STEPS - 1 - 2 * i, x_s, y_s, 0)
        backward(STEPS - 2 - 2 * i, y_s, x_s, 2)
        return carry

    lax.fori_loop(0, STEPS // 2 - 1, backward_pair, 0, unroll=4)
    backward(1, x_s, None, 1)
    y = lax.axis_index("y")
    for d, out_ref in enumerate(out_refs):
        for h in range(WIN // N_Y):
            j = ((y + d - first) & (N_Y - 1)) + N_Y * h
            out_ref[h] = g_s[j] * (lit_ref[0, j].astype(F32) * (-1.0 / STEPS))


def stack_kernel(before_ref, first_ref, second_ref, out_ref):
    out_ref[0 : WIN // N_Y] = first_ref[...]
    out_ref[WIN // N_Y :] = second_ref[...]


def route_kernel(cell_ref, place_ref, *refs):
    gathered, (own_ref, other_ref) = refs[:-2], refs[-2:]
    z, x_own, core_own, y_own = (lax.axis_index(a) for a in AXES)
    own_ref[...] = jnp.zeros_like(own_ref)
    other_ref[...] = jnp.zeros_like(other_ref)
    for i, blocks_ref in enumerate(gathered):
        x = (x_own - X_STEPS[i // 2]) & (N_X - 1)
        for j in range(WIN // 2):
            y = (y_own - (i % 2 * 2 + j // 2)) & (N_Y - 1)
            first = first_block(cell_ref[((z * N_X + x) * N_CORE + core_own) * N_Y + y])
            place = place_ref[first + ((y_own - first) & (N_Y - 1)) + N_Y * (j % 2)]
            slot = (lax.shift_right_logical(place, 3) - z) & (N_Z - 1)
            to_x = lax.shift_right_logical(place, 1) & (N_X - 1)
            to_core = place & (N_CORE - 1)

            @pl.when((to_x == x_own) & (to_core == core_own))
            def _():
                own_ref[slot] = own_ref[slot] + blocks_ref[j]

            @pl.when((to_x == x_own) & (to_core != core_own))
            def _():
                other_ref[slot] = other_ref[slot] + blocks_ref[j]


def join_kernel(own_ref, other_ref, *out_refs):
    for offsets, out_ref in zip(Z_GROUPS, out_refs, strict=True):
        for i, d in enumerate(offsets):
            out_ref[i] = own_ref[d % N_Z] + other_ref[d % N_Z]


def shift(v, axis, size, by):
    return lax.ppermute(v, axis, [(i, (i + by) % size) for i in range(size)])


def ricker(step_number):
    scaled_time = (step_number.astype(F32) - 4.0) * 0.55
    return 2.0 * (1.0 - 2.0 * scaled_time * scaled_time) * jnp.exp(-scaled_time * scaled_time)


def local(courant_sq, start_field, adjoint_state, observed, source_cell, lit_blocks, block_place):
    smem = pl.BlockSpec(memory_space=pltpu.SMEM)
    vmem = pl.BlockSpec(memory_space=pltpu.VMEM)
    hbm = pl.BlockSpec(memory_space=pltpu.HBM)
    plane = pltpu.VMEM((NZ, WIN * BW), F32)
    field = pltpu.VMEM((WIN, NZ, BW), F32)
    parts = pltpu.VMEM((WIN, NZ, 2 * BW), BF16)
    piece = jax.ShapeDtypeStruct((WIN // N_Y, NZ, BW), F32)
    pieces = pl.pallas_call(
        wave_kernel,
        out_shape=(piece,) * N_Y,
        in_specs=[hbm] * 8,
        out_specs=(vmem,) * N_Y,
        scratch_shapes=[
            plane, plane, plane,
            pltpu.VMEM((STEPS, WIN * BW), F32),
            pltpu.VMEM((2 * BW, 2 * BW), BF16),
            pltpu.VMEM((NZ, 2 * NZ), BF16),
            field, field, field,
            pltpu.VMEM((STEPS + 1, WIN, NZ, BW), F32),
            parts, parts,
            pltpu.VMEM((WIN, 8, BW), F32),
            pltpu.VMEM((STEPS + 1, WIN, 8, BW), F32),
            pltpu.SMEM((NB,), jnp.int32),
            pltpu.SMEM((1, WIN), jnp.int32),
            pltpu.SemaphoreType.DMA((8,)),
        ],
        compiler_params=pltpu.CompilerParams(vmem_limit_bytes=58 << 20),
        name="wave",
    )(
        source_cell, lit_blocks, courant_sq, start_field, adjoint_state, observed,
        jnp.asarray(lateral_matrix(), BF16), jnp.asarray(depth_matrix(), BF16),
    )
    near = jnp.concatenate([pieces[0], shift(pieces[1], "y", N_Y, 1)], 0)
    far = pl.pallas_call(
        stack_kernel,
        out_shape=jax.ShapeDtypeStruct((WIN // 2, NZ, BW), F32),
        in_specs=[pl.BlockSpec(memory_space=pl.ANY)] + [vmem] * 2,
        out_specs=vmem,
        compiler_params=pltpu.CompilerParams(vmem_limit_bytes=16 << 20),
        name="stack",
    )(near, shift(pieces[2], "y", N_Y, 2), shift(pieces[3], "y", N_Y, 3))
    near_left, near_right = shift(near, "x", N_X, 1), shift(near, "x", N_X, -1)
    far_left, far_right = shift(far, "x", N_X, 1), shift(far, "x", N_X, -1)
    gathered = (
        near, far, near_left, far_left, near_right, far_right,
        shift(near_left, "x", N_X, 1), shift(far_right, "x", N_X, -1),
    )
    slots = jax.ShapeDtypeStruct((N_Z, NZ, BW), F32)
    own, other = pl.pallas_call(
        route_kernel,
        out_shape=(slots, slots),
        in_specs=[smem] * 2 + [vmem] * len(gathered),
        out_specs=(vmem, vmem),
        compiler_params=pltpu.CompilerParams(vmem_limit_bytes=16 << 20),
        name="route",
    )(source_cell, block_place, *gathered)
    here, up, down, up_three, down_three = pl.pallas_call(
        join_kernel,
        out_shape=tuple(jax.ShapeDtypeStruct((len(g), NZ, BW), F32) for g in Z_GROUPS),
        in_specs=[vmem, vmem],
        out_specs=(vmem,) * len(Z_GROUPS),
        compiler_params=pltpu.CompilerParams(vmem_limit_bytes=16 << 20),
        name="join",
    )(own, shift(other, "core", N_CORE, 1))
    up, down = shift(up, "z", N_Z, 1), shift(down, "z", N_Z, -1)
    up_three = shift(up_three + up[1:2] + down[1:], "z", N_Z, 3)
    down_three = shift(down_three + up[2:], "z", N_Z, -3)
    return (here + up[:1] + down[:1]) + (up_three + down_three)


def solution(mesh):
    split_mesh = Mesh(mesh.devices.reshape(N_Z, N_X, N_CORE, N_Y), AXES)
    split = P(AXES, None, None)
    return jax.shard_map(
        local,
        mesh=split_mesh,
        in_specs=(split, split, split, split, P(), P(AXES, None), P()),
        out_specs=split,
        check_vma=False,
    )
```

```python
import jax
import jax.numpy as jnp
import numpy as np
from jax import lax
from jax.experimental import pallas as pl
from jax.experimental.pallas import tpu as pltpu
from jax.sharding import Mesh, PartitionSpec as P

NZ = 96
BW = 128
WIN = 8
STEPS = 16
NB = 256
N_Z, N_X, N_CORE, N_Y = 8, 4, 2, 4
AXES = ("z", "x", "core", "y")
F32 = jnp.float32
BF16 = jnp.bfloat16

CENTRE, TAPS, REST, SCALE = -28672.0, (8064.0, -1008.0, 128.0, -9.0), -28.0, 5040.0
X_STEPS = (0, 1, -1, 2)
Z_GROUPS = ((0,), (1, 4, -2), (-1, 2), (3,), (-3,))
receiver_row = 2
source_row = 6


def lateral_matrix():
    m = np.zeros((BW, 2 * BW), np.float32)
    for i in range(BW):
        for k in range(-4, 5):
            column = i + k
            weight = TAPS[abs(k) - 1] if k else CENTRE
            if 0 <= column < BW:
                m[i, column] = weight
            else:
                m[i, BW + column % BW] = weight
    return np.concatenate([m, m], 0)


def depth_matrix():
    m = np.zeros((NZ, NZ), np.float32)
    for i in range(NZ):
        for k in range(-4, 5):
            if 0 <= i + k < NZ:
                m[i, i + k] = TAPS[abs(k) - 1] if k else REST
    return np.concatenate([m, m], 1)


def halves(v):
    high = v.astype(BF16)
    return high, v - high.astype(F32)


def block(t):
    return slice(t * BW, (t + 1) * BW)


ROWS = 16
PARTS = [slice(r, r + ROWS) for r in range(0, NZ, ROWS)]


def put_halves(x_ref, t, r, v):
    high, rest = halves(v)
    x_ref[t, r, 0:BW] = high
    x_ref[t, r, BW : 2 * BW] = rest.astype(BF16)


def laplace(x_ref, lateral, depth):
    halves_of_all = x_ref[...].reshape(WIN * NZ, 2 * BW)
    sides = jnp.dot(halves_of_all, lateral, preferred_element_type=F32).reshape(WIN, NZ, 2 * BW)
    deep = []
    for p in range(0, WIN, 2):
        pair = [
            jnp.concatenate([x_ref[p][:, s : s + BW], x_ref[p + 1][:, s : s + BW]], 1)
            for s in (0, BW)
        ]
        deep.append(jnp.dot(depth, jnp.concatenate(pair, 0), preferred_element_type=F32))
    from_left = lax.broadcasted_iota(jnp.int32, (ROWS, BW), 1) < BW // 2
    zeros = jnp.zeros((ROWS, BW), F32)

    def part(t, r):
        spilled = jnp.where(
            from_left,
            sides[t - 1][r, BW:] if t > 0 else zeros,
            sides[t + 1][r, BW:] if t < WIN - 1 else zeros,
        )
        return (sides[t][r, :BW] + deep[t // 2][r, t % 2 * BW : (t % 2 + 1) * BW]) + spilled

    return part


def add_top(v, top):
    return jnp.concatenate([v[0:8] + top, v[8:]], 0)


def first_block(cell):
    return jnp.clip(lax.shift_right_logical(cell, 7) - WIN // 2, 0, NB - WIN)


def own_shot():
    z, x, core, y = (lax.axis_index(a) for a in AXES)
    return ((z * N_X + x) * N_CORE + core) * N_Y + y


def wave_kernel(
    cell_in, lit_in, c_in, u_in, a_in, obs_ref, lateral_ref, depth_ref, *refs
):
    out_refs = refs[:N_Y]
    (c_s, u_s, a_s, obs_s, lat_s, dep_s, q_s, v_s, g_s, hist_s, x_s, y_s, top_s, row_s, cell_ref, lit_ref, sem) = refs[N_Y:]
    copies = [
        pltpu.make_async_copy(src, dst, sem.at[i])
        for i, (src, dst) in enumerate(
            (
                (u_in.at[0], u_s), (lateral_ref, lat_s), (depth_ref, dep_s), (cell_in, cell_ref),
                (c_in.at[0], c_s), (a_in.at[0], a_s), (obs_ref.at[0], obs_s), (lit_in, lit_ref),
            )
        )
    ]
    for copy in copies:
        copy.start()
    for copy in copies[:4]:
        copy.wait()
    cell = cell_ref[own_shot()]
    first = first_block(cell)
    source_column = cell - first * BW
    rows = lax.broadcasted_iota(jnp.int32, (8, BW), 0)
    columns = lax.broadcasted_iota(jnp.int32, (8, BW), 1)
    lateral = lat_s[...]
    depth = dep_s[...]

    def whole_laplace(field):
        for t in range(WIN):
            for r in PARTS:
                high, rest = halves(field[r, block(t)])
                low, last = halves(rest)
                x_s[t, r, 0:BW] = high
                x_s[t, r, BW : 2 * BW] = low
                put_halves(y_s, t, r, last)
        first_part, last_part = laplace(x_s, lateral, depth), laplace(y_s, lateral, depth)
        return lambda t, r: first_part(t, r) + last_part(t, r)

    def source(n, t):
        at_source = (rows == source_row) & (columns + t * BW == source_column)
        return jnp.where(at_source, ricker(jnp.full((8, BW), n, jnp.int32)) * SCALE, 0.0)

    def keep_top(n, t, v):
        top = top_s[t] + v[0:8]
        top_s[t] = top
        row_s[n, t] = top

    part = whole_laplace(u_s)
    copies[4].wait()
    for t in range(WIN):
        top_s[t] = u_s[0:8, block(t)]
        for r in PARTS:
            c = c_s[r, block(t)] * (1.0 / SCALE)
            c_s[r, block(t)] = c
            q = part(t, r)
            q_s[t, r] = q
            v = c * (q if r.start else add_top(q, source(0, t)))
            hist_s[0, t, r] = v
            if not r.start:
                keep_top(0, t, v)
            put_halves(x_s, t, r, v)

    def forward(n, x_ref, next_ref):
        part = laplace(x_ref, lateral, depth)
        for t in range(WIN):
            for r in PARTS:
                q = q_s[t, r] + part(t, r)
                q_s[t, r] = q
                if not r.start:
                    q = add_top(q, source(n, t))
                v = hist_s[n - 1, t, r] + c_s[r, block(t)] * q
                hist_s[n, t, r] = v
                if not r.start:
                    keep_top(n, t, v)
                put_halves(next_ref, t, r, v)

    def forward_pair(i, carry):
        forward(2 * i + 1, x_s, y_s)
        forward(2 * i + 2, y_s, x_s)
        return carry

    lax.fori_loop(0, STEPS // 2, forward_pair, 0, unroll=STEPS // 2)
    for copy in copies[5:]:
        copy.wait()
    for n in range(STEPS):
        for t in range(WIN):
            misfit = row_s[n, t] - obs_s[n : n + 1, block(t)]
            row_s[n, t] = jnp.where(rows == receiver_row, misfit, 0.0) * SCALE
    part = whole_laplace(a_s)
    for t in range(WIN):
        for r in PARTS:
            q = part(t, r)
            q_s[t, r] = q
            w = c_s[r, block(t)] * (q if r.start else add_top(q, row_s[STEPS - 1, t]))
            v_s[t, r] = w
            g_s[t, r] = (a_s[r, block(t)] + w) * (hist_s[STEPS, t, r] - hist_s[0, t, r])
            put_halves(x_s, t, r, w)

    def backward(n, x_ref, next_ref, image):
        part = laplace(x_ref, lateral, depth)
        for t in range(WIN):
            for r in PARTS:
                q = q_s[t, r] + part(t, r)
                if next_ref is not None:
                    q_s[t, r] = q
                if not r.start:
                    q = add_top(q, row_s[n - 1, t])
                before = v_s[t, r]
                w = before + c_s[r, block(t)] * q
                v_s[t, r] = w
                if image:
                    image_sum = g_s[t, r] + w * (hist_s[n, t, r] - hist_s[0, t, r])
                    if image == 2:
                        later = before * (hist_s[n + 1, t, r] - hist_s[0, t, r])
                        image_sum = image_sum + later
                    g_s[t, r] = image_sum
                if next_ref is not None:
                    put_halves(next_ref, t, r, w)

    def backward_pair(i, carry):
        backward(STEPS - 1 - 2 * i, x_s, y_s, 0)
        backward(STEPS - 2 - 2 * i, y_s, x_s, 2)
        return carry

    lax.fori_loop(0, STEPS // 2 - 1, backward_pair, 0, unroll=STEPS // 2 - 1)
    backward(1, x_s, None, 1)
    y = lax.axis_index("y")
    for d, out_ref in enumerate(out_refs):
        for h in range(WIN // N_Y):
            j = ((y + d - first) & (N_Y - 1)) + N_Y * h
            out_ref[h] = g_s[j] * (lit_ref[0, j].astype(F32) * (-1.0 / STEPS))


def stack_kernel(before_ref, first_ref, second_ref, out_ref):
    out_ref[0 : WIN // N_Y] = first_ref[...]
    out_ref[WIN // N_Y :] = second_ref[...]


def route_kernel(cell_ref, place_ref, *refs):
    gathered, (own_ref, other_ref) = refs[:-2], refs[-2:]
    z, x_own, core_own, y_own = (lax.axis_index(a) for a in AXES)
    own_ref[...] = jnp.zeros_like(own_ref)
    other_ref[...] = jnp.zeros_like(other_ref)
    for i, blocks_ref in enumerate(gathered):
        x = (x_own - X_STEPS[i // 2]) & (N_X - 1)
        for j in range(WIN // 2):
            y = (y_own - (i % 2 * 2 + j // 2)) & (N_Y - 1)
            first = first_block(cell_ref[((z * N_X + x) * N_CORE + core_own) * N_Y + y])
            place = place_ref[first + ((y_own - first) & (N_Y - 1)) + N_Y * (j % 2)]
            slot = (lax.shift_right_logical(place, 3) - z) & (N_Z - 1)
            to_x = lax.shift_right_logical(place, 1) & (N_X - 1)
            to_core = place & (N_CORE - 1)

            @pl.when((to_x == x_own) & (to_core == core_own))
            def _():
                own_ref[slot] = own_ref[slot] + blocks_ref[j]

            @pl.when((to_x == x_own) & (to_core != core_own))
            def _():
                other_ref[slot] = other_ref[slot] + blocks_ref[j]


def join_kernel(own_ref, other_ref, *out_refs):
    for offsets, out_ref in zip(Z_GROUPS, out_refs, strict=True):
        for i, d in enumerate(offsets):
            out_ref[i] = own_ref[d % N_Z] + other_ref[d % N_Z]


def shift(v, axis, size, by):
    return lax.ppermute(v, axis, [(i, (i + by) % size) for i in range(size)])


def ricker(step_number):
    scaled_time = (step_number.astype(F32) - 4.0) * 0.55
    return 2.0 * (1.0 - 2.0 * scaled_time * scaled_time) * jnp.exp(-scaled_time * scaled_time)


def local(courant_sq, start_field, adjoint_state, observed, source_cell, lit_blocks, block_place):
    smem = pl.BlockSpec(memory_space=pltpu.SMEM)
    vmem = pl.BlockSpec(memory_space=pltpu.VMEM)
    hbm = pl.BlockSpec(memory_space=pltpu.HBM)
    plane = pltpu.VMEM((NZ, WIN * BW), F32)
    field = pltpu.VMEM((WIN, NZ, BW), F32)
    parts = pltpu.VMEM((WIN, NZ, 2 * BW), BF16)
    piece = jax.ShapeDtypeStruct((WIN // N_Y, NZ, BW), F32)
    pieces = pl.pallas_call(
        wave_kernel,
        out_shape=(piece,) * N_Y,
        in_specs=[hbm] * 8,
        out_specs=(vmem,) * N_Y,
        scratch_shapes=[
            plane, plane, plane,
            pltpu.VMEM((STEPS, WIN * BW), F32),
            pltpu.VMEM((2 * BW, 2 * BW), BF16),
            pltpu.VMEM((NZ, 2 * NZ), BF16),
            field, field, field,
            pltpu.VMEM((STEPS + 1, WIN, NZ, BW), F32),
            parts, parts,
            pltpu.VMEM((WIN, 8, BW), F32),
            pltpu.VMEM((STEPS + 1, WIN, 8, BW), F32),
            pltpu.SMEM((NB,), jnp.int32),
            pltpu.SMEM((1, WIN), jnp.int32),
            pltpu.SemaphoreType.DMA((8,)),
        ],
        compiler_params=pltpu.CompilerParams(vmem_limit_bytes=58 << 20),
        name="wave",
    )(
        source_cell, lit_blocks, courant_sq, start_field, adjoint_state, observed,
        jnp.asarray(lateral_matrix(), BF16), jnp.asarray(depth_matrix(), BF16),
    )
    near = jnp.concatenate([pieces[0], shift(pieces[1], "y", N_Y, 1)], 0)
    far = pl.pallas_call(
        stack_kernel,
        out_shape=jax.ShapeDtypeStruct((WIN // 2, NZ, BW), F32),
        in_specs=[pl.BlockSpec(memory_space=pl.ANY)] + [vmem] * 2,
        out_specs=vmem,
        compiler_params=pltpu.CompilerParams(vmem_limit_bytes=16 << 20),
        name="stack",
    )(near, shift(pieces[2], "y", N_Y, 2), shift(pieces[3], "y", N_Y, 3))
    near_left, near_right = shift(near, "x", N_X, 1), shift(near, "x", N_X, -1)
    far_left, far_right = shift(far, "x", N_X, 1), shift(far, "x", N_X, -1)
    gathered = (
        near, far, near_left, far_left, near_right, far_right,
        shift(near_left, "x", N_X, 1), shift(far_right, "x", N_X, -1),
    )
    slots = jax.ShapeDtypeStruct((N_Z, NZ, BW), F32)
    own, other = pl.pallas_call(
        route_kernel,
        out_shape=(slots, slots),
        in_specs=[smem] * 2 + [vmem] * len(gathered),
        out_specs=(vmem, vmem),
        compiler_params=pltpu.CompilerParams(vmem_limit_bytes=16 << 20),
        name="route",
    )(source_cell, block_place, *gathered)
    here, up, down, up_three, down_three = pl.pallas_call(
        join_kernel,
        out_shape=tuple(jax.ShapeDtypeStruct((len(g), NZ, BW), F32) for g in Z_GROUPS),
        in_specs=[vmem, vmem],
        out_specs=(vmem,) * len(Z_GROUPS),
        compiler_params=pltpu.CompilerParams(vmem_limit_bytes=16 << 20),
        name="join",
    )(own, shift(other, "core", N_CORE, 1))
    up, down = shift(up, "z", N_Z, 1), shift(down, "z", N_Z, -1)
    up_three = shift(up_three + up[1:2] + down[1:], "z", N_Z, 3)
    down_three = shift(down_three + up[2:], "z", N_Z, -3)
    return (here + up[:1] + down[:1]) + (up_three + down_three)


def solution(mesh):
    split_mesh = Mesh(mesh.devices.reshape(N_Z, N_X, N_CORE, N_Y), AXES)
    split = P(AXES, None, None)
    return jax.shard_map(
        local,
        mesh=split_mesh,
        in_specs=(split, split, split, split, P(), P(AXES, None), P()),
        out_specs=split,
        check_vma=False,
    )
```

```python
import jax
import jax.numpy as jnp
import numpy as np
from jax import lax
from jax.experimental import pallas as pl
from jax.experimental.pallas import tpu as pltpu
from jax.sharding import Mesh, PartitionSpec as P

NZ = 96
BW = 128
WIN = 8
STEPS = 16
NB = 256
N_Z, N_X, N_CORE, N_Y = 8, 4, 2, 4
AXES = ("z", "x", "core", "y")
F32 = jnp.float32
BF16 = jnp.bfloat16

CENTRE, TAPS, REST, SCALE = -28672.0, (8064.0, -1008.0, 128.0, -9.0), -28.0, 5040.0
X_STEPS = (0, 1, -1, 2)
Z_GROUPS = ((0,), (1, 4, -2), (-1, 2), (3,), (-3,))
receiver_row = 2
source_row = 6


def lateral_matrix():
    m = np.zeros((BW, 2 * BW), np.float32)
    for i in range(BW):
        for k in range(-4, 5):
            column = i + k
            weight = TAPS[abs(k) - 1] if k else CENTRE
            if 0 <= column < BW:
                m[i, column] = weight
            else:
                m[i, BW + column % BW] = weight
    return np.concatenate([m, m], 0)


def depth_matrix():
    m = np.zeros((NZ, NZ), np.float32)
    for i in range(NZ):
        for k in range(-4, 5):
            if 0 <= i + k < NZ:
                m[i, i + k] = TAPS[abs(k) - 1] if k else REST
    return np.concatenate([m, m], 1)


def halves(v):
    high = v.astype(BF16)
    return high, v - high.astype(F32)


def block(t):
    return slice(t * BW, (t + 1) * BW)


ROWS = 16
PARTS = [slice(r, r + ROWS) for r in range(0, NZ, ROWS)]


def put_halves(x_ref, t, r, v):
    high, rest = halves(v)
    x_ref[t, r, 0:BW] = high
    x_ref[t, r, BW : 2 * BW] = rest.astype(BF16)


def laplace(x_ref, lateral, depth):
    halves_of_all = x_ref[...].reshape(WIN * NZ, 2 * BW)
    sides = jnp.dot(halves_of_all, lateral, preferred_element_type=F32).reshape(WIN, NZ, 2 * BW)
    deep = []
    for p in range(0, WIN, 2):
        pair = [
            jnp.concatenate([x_ref[p][:, s : s + BW], x_ref[p + 1][:, s : s + BW]], 1)
            for s in (0, BW)
        ]
        deep.append(jnp.dot(depth, jnp.concatenate(pair, 0), preferred_element_type=F32))
    from_left = lax.broadcasted_iota(jnp.int32, (ROWS, BW), 1) < BW // 2
    zeros = jnp.zeros((ROWS, BW), F32)

    def part(t, r):
        spilled = jnp.where(
            from_left,
            sides[t - 1][r, BW:] if t > 0 else zeros,
            sides[t + 1][r, BW:] if t < WIN - 1 else zeros,
        )
        return (sides[t][r, :BW] + deep[t // 2][r, t % 2 * BW : (t % 2 + 1) * BW]) + spilled

    return part


def add_top(v, top):
    return jnp.concatenate([v[0:8] + top, v[8:]], 0)


def first_block(cell):
    return jnp.clip(lax.shift_right_logical(cell, 7) - WIN // 2, 0, NB - WIN)


def own_shot():
    z, x, core, y = (lax.axis_index(a) for a in AXES)
    return ((z * N_X + x) * N_CORE + core) * N_Y + y


def wave_kernel(
    cell_in, place_in, lit_in, c_in, u_in, a_in, obs_ref, lateral_ref, depth_ref, *refs
):
    out_refs, table_ref = refs[:N_Y], refs[N_Y]
    (c_s, u_s, a_s, obs_s, lat_s, dep_s, q_s, v_s, g_s, hist_s, x_s, y_s, top_s, row_s, cell_ref, place_ref, lit_ref, sem) = refs[N_Y + 1 :]
    copies = [
        pltpu.make_async_copy(src, dst, sem.at[i])
        for i, (src, dst) in enumerate(
            (
                (u_in.at[0], u_s), (lateral_ref, lat_s), (depth_ref, dep_s), (cell_in, cell_ref),
                (c_in.at[0], c_s), (a_in.at[0], a_s), (obs_ref.at[0], obs_s), (lit_in, lit_ref),
                (place_in, place_ref),
            )
        )
    ]
    for copy in copies:
        copy.start()
    for copy in copies[:4]:
        copy.wait()
    cell = cell_ref[own_shot()]
    first = first_block(cell)
    source_column = cell - first * BW
    rows = lax.broadcasted_iota(jnp.int32, (8, BW), 0)
    columns = lax.broadcasted_iota(jnp.int32, (8, BW), 1)
    lateral = lat_s[...]
    depth = dep_s[...]

    def whole_laplace(field):
        for t in range(WIN):
            for r in PARTS:
                high, rest = halves(field[r, block(t)])
                low, last = halves(rest)
                x_s[t, r, 0:BW] = high
                x_s[t, r, BW : 2 * BW] = low
                put_halves(y_s, t, r, last)
        first_part, last_part = laplace(x_s, lateral, depth), laplace(y_s, lateral, depth)
        return lambda t, r: first_part(t, r) + last_part(t, r)

    def source(n, t):
        at_source = (rows == source_row) & (columns + t * BW == source_column)
        return jnp.where(at_source, ricker(jnp.full((8, BW), n, jnp.int32)) * SCALE, 0.0)

    def keep_top(n, t, v):
        top = top_s[t] + v[0:8]
        top_s[t] = top
        row_s[n, t] = top

    part = whole_laplace(u_s)
    copies[4].wait()
    for t in range(WIN):
        top_s[t] = u_s[0:8, block(t)]
        for r in PARTS:
            c = c_s[r, block(t)] * (1.0 / SCALE)
            c_s[r, block(t)] = c
            q = part(t, r)
            q_s[t, r] = q
            v = c * (q if r.start else add_top(q, source(0, t)))
            hist_s[0, t, r] = v
            if not r.start:
                keep_top(0, t, v)
            put_halves(x_s, t, r, v)

    def forward(n, x_ref, next_ref):
        part = laplace(x_ref, lateral, depth)
        for t in range(WIN):
            for r in PARTS:
                q = q_s[t, r] + part(t, r)
                q_s[t, r] = q
                if not r.start:
                    q = add_top(q, source(n, t))
                v = hist_s[n - 1, t, r] + c_s[r, block(t)] * q
                hist_s[n, t, r] = v
                if not r.start:
                    keep_top(n, t, v)
                put_halves(next_ref, t, r, v)

    def forward_pair(i, carry):
        forward(2 * i + 1, x_s, y_s)
        forward(2 * i + 2, y_s, x_s)
        return carry

    lax.fori_loop(0, STEPS // 2, forward_pair, 0, unroll=STEPS // 2)
    for copy in copies[5:]:
        copy.wait()
    fill_table(cell_ref, place_ref, table_ref)
    for n in range(STEPS):
        for t in range(WIN):
            misfit = row_s[n, t] - obs_s[n : n + 1, block(t)]
            row_s[n, t] = jnp.where(rows == receiver_row, misfit, 0.0) * SCALE
    part = whole_laplace(a_s)
    for t in range(WIN):
        for r in PARTS:
            q = part(t, r)
            q_s[t, r] = q
            w = c_s[r, block(t)] * (q if r.start else add_top(q, row_s[STEPS - 1, t]))
            v_s[t, r] = w
            g_s[t, r] = (a_s[r, block(t)] + w) * (hist_s[STEPS, t, r] - hist_s[0, t, r])
            put_halves(x_s, t, r, w)

    def backward(n, x_ref, next_ref, image):
        part = laplace(x_ref, lateral, depth)
        for t in range(WIN):
            for r in PARTS:
                q = q_s[t, r] + part(t, r)
                if next_ref is not None:
                    q_s[t, r] = q
                if not r.start:
                    q = add_top(q, row_s[n - 1, t])
                before = v_s[t, r]
                w = before + c_s[r, block(t)] * q
                v_s[t, r] = w
                if image:
                    image_sum = g_s[t, r] + w * (hist_s[n, t, r] - hist_s[0, t, r])
                    if image == 2:
                        later = before * (hist_s[n + 1, t, r] - hist_s[0, t, r])
                        image_sum = image_sum + later
                    g_s[t, r] = image_sum
                if next_ref is not None:
                    put_halves(next_ref, t, r, w)

    def backward_pair(i, carry):
        backward(STEPS - 1 - 2 * i, x_s, y_s, 0)
        backward(STEPS - 2 - 2 * i, y_s, x_s, 2)
        return carry

    lax.fori_loop(0, STEPS // 2 - 1, backward_pair, 0, unroll=STEPS // 2 - 1)
    backward(1, x_s, None, 1)
    y = lax.axis_index("y")
    for d, out_ref in enumerate(out_refs):
        for h in range(WIN // N_Y):
            j = ((y + d - first) & (N_Y - 1)) + N_Y * h
            out_ref[h] = g_s[j] * (lit_ref[0, j].astype(F32) * (-1.0 / STEPS))


def stack_kernel(before_ref, first_ref, second_ref, out_ref):
    out_ref[0 : WIN // N_Y] = first_ref[...]
    out_ref[WIN // N_Y :] = second_ref[...]


def fill_table(cell_ref, place_ref, table_ref):
    z, x_own, core_own, y_own = (lax.axis_index(a) for a in AXES)
    for i in range(len(X_STEPS) * N_Y):
        x = (x_own - X_STEPS[i // N_Y]) & (N_X - 1)
        y = (y_own - i % N_Y) & (N_Y - 1)
        first = first_block(cell_ref[((z * N_X + x) * N_CORE + core_own) * N_Y + y])
        k = first + ((y_own - first) & (N_Y - 1))
        for h in range(WIN // N_Y):
            place = place_ref[k + N_Y * h]
            slot = (lax.shift_right_logical(place, 3) - z) & (N_Z - 1)
            to_x = lax.shift_right_logical(place, 1) & (N_X - 1)
            crosses = (place & (N_CORE - 1)) ^ core_own
            table_ref[2 * i + h] = jnp.where(to_x == x_own, slot + N_Z * crosses, -1)


def route_kernel(table_ref, *refs):
    gathered, (own_ref, other_ref) = refs[:-2], refs[-2:]
    own_ref[...] = jnp.zeros_like(own_ref)
    other_ref[...] = jnp.zeros_like(other_ref)
    for i, blocks_ref in enumerate(gathered):
        for j in range(WIN // 2):
            slot = table_ref[i * (WIN // 2) + j]

            @pl.when((slot >= 0) & (slot < N_Z))
            def _():
                own_ref[slot] = own_ref[slot] + blocks_ref[j]

            @pl.when(slot >= N_Z)
            def _():
                other_ref[slot - N_Z] = other_ref[slot - N_Z] + blocks_ref[j]


def join_kernel(own_ref, other_ref, *out_refs):
    for offsets, out_ref in zip(Z_GROUPS, out_refs, strict=True):
        for i, d in enumerate(offsets):
            out_ref[i] = own_ref[d % N_Z] + other_ref[d % N_Z]


def shift(v, axis, size, by):
    return lax.ppermute(v, axis, [(i, (i + by) % size) for i in range(size)])


def ricker(step_number):
    scaled_time = (step_number.astype(F32) - 4.0) * 0.55
    return 2.0 * (1.0 - 2.0 * scaled_time * scaled_time) * jnp.exp(-scaled_time * scaled_time)


def local(courant_sq, start_field, adjoint_state, observed, source_cell, lit_blocks, block_place):
    smem = pl.BlockSpec(memory_space=pltpu.SMEM)
    vmem = pl.BlockSpec(memory_space=pltpu.VMEM)
    hbm = pl.BlockSpec(memory_space=pltpu.HBM)
    plane = pltpu.VMEM((NZ, WIN * BW), F32)
    field = pltpu.VMEM((WIN, NZ, BW), F32)
    parts = pltpu.VMEM((WIN, NZ, 2 * BW), BF16)
    piece = jax.ShapeDtypeStruct((WIN // N_Y, NZ, BW), F32)
    *pieces, table = pl.pallas_call(
        wave_kernel,
        out_shape=(piece,) * N_Y + (jax.ShapeDtypeStruct((len(X_STEPS) * WIN,), jnp.int32),),
        in_specs=[hbm] * 9,
        out_specs=(vmem,) * N_Y + (smem,),
        scratch_shapes=[
            plane, plane, plane,
            pltpu.VMEM((STEPS, WIN * BW), F32),
            pltpu.VMEM((2 * BW, 2 * BW), BF16),
            pltpu.VMEM((NZ, 2 * NZ), BF16),
            field, field, field,
            pltpu.VMEM((STEPS + 1, WIN, NZ, BW), F32),
            parts, parts,
            pltpu.VMEM((WIN, 8, BW), F32),
            pltpu.VMEM((STEPS + 1, WIN, 8, BW), F32),
            pltpu.SMEM((NB,), jnp.int32),
            pltpu.SMEM((NB,), jnp.int32),
            pltpu.SMEM((1, WIN), jnp.int32),
            pltpu.SemaphoreType.DMA((9,)),
        ],
        compiler_params=pltpu.CompilerParams(vmem_limit_bytes=58 << 20),
        name="wave",
    )(
        source_cell, block_place, lit_blocks, courant_sq, start_field, adjoint_state, observed,
        jnp.asarray(lateral_matrix(), BF16), jnp.asarray(depth_matrix(), BF16),
    )
    from_second, from_third = shift(pieces[2], "y", N_Y, 2), shift(pieces[3], "y", N_Y, 3)
    near = jnp.concatenate([pieces[0], shift(pieces[1], "y", N_Y, 1)], 0)
    far = pl.pallas_call(
        stack_kernel,
        out_shape=jax.ShapeDtypeStruct((WIN // 2, NZ, BW), F32),
        in_specs=[pl.BlockSpec(memory_space=pl.ANY)] + [vmem] * 2,
        out_specs=vmem,
        compiler_params=pltpu.CompilerParams(vmem_limit_bytes=16 << 20),
        name="stack",
    )(near, from_second, from_third)
    near_left, near_right = shift(near, "x", N_X, 1), shift(near, "x", N_X, -1)
    far_left, far_right = shift(far, "x", N_X, 1), shift(far, "x", N_X, -1)
    gathered = (
        near, far, near_left, far_left, near_right, far_right,
        shift(near_left, "x", N_X, 1), shift(far_right, "x", N_X, -1),
    )
    slots = jax.ShapeDtypeStruct((N_Z, NZ, BW), F32)
    own, other = pl.pallas_call(
        route_kernel,
        out_shape=(slots, slots),
        in_specs=[smem] + [vmem] * len(gathered),
        out_specs=(vmem, vmem),
        compiler_params=pltpu.CompilerParams(vmem_limit_bytes=16 << 20),
        name="route",
    )(table, *gathered)
    here, up, down, up_three, down_three = pl.pallas_call(
        join_kernel,
        out_shape=tuple(jax.ShapeDtypeStruct((len(g), NZ, BW), F32) for g in Z_GROUPS),
        in_specs=[vmem, vmem],
        out_specs=(vmem,) * len(Z_GROUPS),
        compiler_params=pltpu.CompilerParams(vmem_limit_bytes=16 << 20),
        name="join",
    )(own, shift(other, "core", N_CORE, 1))
    up, down = shift(up, "z", N_Z, 1), shift(down, "z", N_Z, -1)
    up_three = shift(up_three + up[1:2] + down[1:], "z", N_Z, 3)
    down_three = shift(down_three + up[2:], "z", N_Z, -3)
    return (here + up[:1] + down[:1]) + (up_three + down_three)


def solution(mesh):
    split_mesh = Mesh(mesh.devices.reshape(N_Z, N_X, N_CORE, N_Y), AXES)
    split = P(AXES, None, None)
    return jax.shard_map(
        local,
        mesh=split_mesh,
        in_specs=(split, split, split, split, P(), P(AXES, None), P()),
        out_specs=split,
        check_vma=False,
    )
```

```python
import functools

import jax
import jax.numpy as jnp
import numpy as np
from jax import lax
from jax.experimental import pallas as pl
from jax.experimental.pallas import tpu as pltpu
from jax.sharding import Mesh, PartitionSpec as P

NZ = 96
BW = 128
WIN = 8
STEPS = 16
NB = 256
N_Z, N_X, N_CORE, N_Y = 8, 4, 2, 4
AXES = ("z", "x", "core", "y")
F32 = jnp.float32
BF16 = jnp.bfloat16

CENTRE, TAPS, REST, SCALE = -28672.0, (8064.0, -1008.0, 128.0, -9.0), -28.0, 5040.0
X_STEPS = (0, 1, -1, 2)
Z_GROUPS = ((0,), (1, 4, -2), (-1, 2), (3,), (-3,))
receiver_row = 2
source_row = 6


def lateral_matrix():
    m = np.zeros((BW, 2 * BW), np.float32)
    for i in range(BW):
        for k in range(-4, 5):
            column = i + k
            weight = TAPS[abs(k) - 1] if k else CENTRE
            if 0 <= column < BW:
                m[i, column] = weight
            else:
                m[i, BW + column % BW] = weight
    return np.concatenate([m, m], 0)


def depth_matrix():
    m = np.zeros((NZ, NZ), np.float32)
    for i in range(NZ):
        for k in range(-4, 5):
            if 0 <= i + k < NZ:
                m[i, i + k] = TAPS[abs(k) - 1] if k else REST
    return np.concatenate([m, m], 1)


def halves(v):
    high = v.astype(BF16)
    return high, v - high.astype(F32)


def block(t):
    return slice(t * BW, (t + 1) * BW)


ROWS = 16
PARTS = [slice(r, r + ROWS) for r in range(0, NZ, ROWS)]


def put_halves(x_ref, t, r, v):
    high, rest = halves(v)
    x_ref[t, r, 0:BW] = high
    x_ref[t, r, BW : 2 * BW] = rest.astype(BF16)


def laplace(x_ref, lateral, depth):
    halves_of_all = x_ref[...].reshape(WIN * NZ, 2 * BW)
    sides = jnp.dot(halves_of_all, lateral, preferred_element_type=F32).reshape(WIN, NZ, 2 * BW)
    deep = []
    for p in range(0, WIN, 2):
        pair = [
            jnp.concatenate([x_ref[p][:, s : s + BW], x_ref[p + 1][:, s : s + BW]], 1)
            for s in (0, BW)
        ]
        deep.append(jnp.dot(depth, jnp.concatenate(pair, 0), preferred_element_type=F32))
    from_left = lax.broadcasted_iota(jnp.int32, (ROWS, BW), 1) < BW // 2
    zeros = jnp.zeros((ROWS, BW), F32)

    def part(t, r):
        spilled = jnp.where(
            from_left,
            sides[t - 1][r, BW:] if t > 0 else zeros,
            sides[t + 1][r, BW:] if t < WIN - 1 else zeros,
        )
        return (sides[t][r, :BW] + deep[t // 2][r, t % 2 * BW : (t % 2 + 1) * BW]) + spilled

    return part


def add_top(v, top):
    return jnp.concatenate([v[0:8] + top, v[8:]], 0)


def first_block(cell):
    return jnp.clip(lax.shift_right_logical(cell, 7) - WIN // 2, 0, NB - WIN)


def own_shot():
    z, x, core, y = (lax.axis_index(a) for a in AXES)
    return ((z * N_X + x) * N_CORE + core) * N_Y + y


def wave_kernel(
    cell_in, place_in, lit_in, c_in, u_in, a_in, obs_ref, lateral_ref, depth_ref, *refs
):
    out_refs, table_ref = refs[:N_Y], refs[N_Y]
    (c_s, u_s, a_s, obs_s, lat_s, dep_s, q_s, v_s, g_s, hist_s, x_s, y_s, top_s, row_s, cell_ref, place_ref, lit_ref, sem) = refs[N_Y + 1 :]
    copies = [
        pltpu.make_async_copy(src, dst, sem.at[i])
        for i, (src, dst) in enumerate(
            (
                (u_in.at[0], u_s), (lateral_ref, lat_s), (depth_ref, dep_s), (cell_in, cell_ref),
                (c_in.at[0], c_s), (a_in.at[0], a_s), (obs_ref.at[0], obs_s), (lit_in, lit_ref),
                (place_in, place_ref),
            )
        )
    ]
    for copy in copies:
        copy.start()
    for copy in copies[:4]:
        copy.wait()
    cell = cell_ref[own_shot()]
    first = first_block(cell)
    source_column = cell - first * BW
    rows = lax.broadcasted_iota(jnp.int32, (8, BW), 0)
    columns = lax.broadcasted_iota(jnp.int32, (8, BW), 1)
    lateral = lat_s[...]
    depth = dep_s[...]

    def whole_laplace(field):
        for t in range(WIN):
            for r in PARTS:
                high, rest = halves(field[r, block(t)])
                low, last = halves(rest)
                x_s[t, r, 0:BW] = high
                x_s[t, r, BW : 2 * BW] = low
                put_halves(y_s, t, r, last)
        first_part, last_part = laplace(x_s, lateral, depth), laplace(y_s, lateral, depth)
        return lambda t, r: first_part(t, r) + last_part(t, r)

    def source(n, t):
        at_source = (rows == source_row) & (columns + t * BW == source_column)
        return jnp.where(at_source, ricker(jnp.full((8, BW), n, jnp.int32)) * SCALE, 0.0)

    def keep_top(n, t, v):
        top = top_s[t] + v[0:8]
        top_s[t] = top
        row_s[n, t] = top

    part = whole_laplace(u_s)
    copies[4].wait()
    for t in range(WIN):
        top_s[t] = u_s[0:8, block(t)]
        for r in PARTS:
            c = c_s[r, block(t)] * (1.0 / SCALE)
            c_s[r, block(t)] = c
            q = part(t, r)
            q_s[t, r] = q
            v = c * (q if r.start else add_top(q, source(0, t)))
            hist_s[0, t, r] = v
            if not r.start:
                keep_top(0, t, v)
            put_halves(x_s, t, r, v)

    def forward(n, x_ref, next_ref):
        part = laplace(x_ref, lateral, depth)
        for t in range(WIN):
            for r in PARTS:
                q = q_s[t, r] + part(t, r)
                q_s[t, r] = q
                if not r.start:
                    q = add_top(q, source(n, t))
                v = hist_s[n - 1, t, r] + c_s[r, block(t)] * q
                hist_s[n, t, r] = v
                if not r.start:
                    keep_top(n, t, v)
                put_halves(next_ref, t, r, v)

    def forward_pair(i, carry):
        forward(2 * i + 1, x_s, y_s)
        forward(2 * i + 2, y_s, x_s)
        return carry

    lax.fori_loop(0, STEPS // 2, forward_pair, 0, unroll=STEPS // 2)
    for copy in copies[5:]:
        copy.wait()
    fill_table(cell_ref, place_ref, table_ref)
    for n in range(STEPS):
        for t in range(WIN):
            misfit = row_s[n, t] - obs_s[n : n + 1, block(t)]
            row_s[n, t] = jnp.where(rows == receiver_row, misfit, 0.0) * SCALE
    part = whole_laplace(a_s)
    for t in range(WIN):
        for r in PARTS:
            q = part(t, r)
            q_s[t, r] = q
            w = c_s[r, block(t)] * (q if r.start else add_top(q, row_s[STEPS - 1, t]))
            v_s[t, r] = w
            g_s[t, r] = (a_s[r, block(t)] + w) * (hist_s[STEPS, t, r] - hist_s[0, t, r])
            put_halves(x_s, t, r, w)

    def backward(n, x_ref, next_ref, image):
        part = laplace(x_ref, lateral, depth)
        for t in range(WIN):
            for r in PARTS:
                q = q_s[t, r] + part(t, r)
                if next_ref is not None:
                    q_s[t, r] = q
                if not r.start:
                    q = add_top(q, row_s[n - 1, t])
                before = v_s[t, r]
                w = before + c_s[r, block(t)] * q
                v_s[t, r] = w
                if image:
                    image_sum = g_s[t, r] + w * (hist_s[n, t, r] - hist_s[0, t, r])
                    if image == 2:
                        later = before * (hist_s[n + 1, t, r] - hist_s[0, t, r])
                        image_sum = image_sum + later
                    g_s[t, r] = image_sum
                if next_ref is not None:
                    put_halves(next_ref, t, r, w)

    def backward_pair(i, carry):
        backward(STEPS - 1 - 2 * i, x_s, y_s, 0)
        backward(STEPS - 2 - 2 * i, y_s, x_s, 2)
        return carry

    lax.fori_loop(0, STEPS // 2 - 1, backward_pair, 0, unroll=STEPS // 2 - 1)
    backward(1, x_s, None, 1)
    y = lax.axis_index("y")
    for d, out_ref in enumerate(out_refs):
        for h in range(WIN // N_Y):
            j = ((y + d - first) & (N_Y - 1)) + N_Y * h
            out_ref[h] = g_s[j] * (lit_ref[0, j].astype(F32) * (-1.0 / STEPS))


def stack_kernel(before_ref, first_ref, second_ref, out_ref):
    out_ref[0 : WIN // N_Y] = first_ref[...]
    out_ref[WIN // N_Y :] = second_ref[...]


def fill_table(cell_ref, place_ref, table_ref):
    z, x_own, core_own, y_own = (lax.axis_index(a) for a in AXES)
    for i in range(len(X_STEPS) * N_Y):
        x = (x_own - X_STEPS[i // N_Y]) & (N_X - 1)
        y = (y_own - i % N_Y) & (N_Y - 1)
        first = first_block(cell_ref[((z * N_X + x) * N_CORE + core_own) * N_Y + y])
        k = first + ((y_own - first) & (N_Y - 1))
        for h in range(WIN // N_Y):
            place = place_ref[k + N_Y * h]
            slot = (lax.shift_right_logical(place, 3) - z) & (N_Z - 1)
            to_x = lax.shift_right_logical(place, 1) & (N_X - 1)
            crosses = (place & (N_CORE - 1)) ^ core_own
            table_ref[2 * i + h] = jnp.where(to_x == x_own, slot + N_Z * crosses, -1)


def route_kernel(lowest, table_ref, *refs):
    gathered, slots_ref = refs[:-1], refs[-1]
    slots_ref[...] = jnp.zeros_like(slots_ref)
    for i, blocks_ref in enumerate(gathered):
        for j in range(WIN // 2):
            slot = table_ref[i * (WIN // 2) + j] - lowest

            @pl.when((slot >= 0) & (slot < N_Z))
            def _():
                slots_ref[slot] = slots_ref[slot] + blocks_ref[j]


def join_kernel(own_ref, other_ref, *out_refs):
    for offsets, out_ref in zip(Z_GROUPS, out_refs, strict=True):
        for i, d in enumerate(offsets):
            out_ref[i] = own_ref[d % N_Z] + other_ref[d % N_Z]


def shift(v, axis, size, by):
    return lax.ppermute(v, axis, [(i, (i + by) % size) for i in range(size)])


def ricker(step_number):
    scaled_time = (step_number.astype(F32) - 4.0) * 0.55
    return 2.0 * (1.0 - 2.0 * scaled_time * scaled_time) * jnp.exp(-scaled_time * scaled_time)


def local(courant_sq, start_field, adjoint_state, observed, source_cell, lit_blocks, block_place):
    smem = pl.BlockSpec(memory_space=pltpu.SMEM)
    vmem = pl.BlockSpec(memory_space=pltpu.VMEM)
    hbm = pl.BlockSpec(memory_space=pltpu.HBM)
    plane = pltpu.VMEM((NZ, WIN * BW), F32)
    field = pltpu.VMEM((WIN, NZ, BW), F32)
    parts = pltpu.VMEM((WIN, NZ, 2 * BW), BF16)
    piece = jax.ShapeDtypeStruct((WIN // N_Y, NZ, BW), F32)
    *pieces, table = pl.pallas_call(
        wave_kernel,
        out_shape=(piece,) * N_Y + (jax.ShapeDtypeStruct((len(X_STEPS) * WIN,), jnp.int32),),
        in_specs=[hbm] * 9,
        out_specs=(vmem,) * N_Y + (smem,),
        scratch_shapes=[
            plane, plane, plane,
            pltpu.VMEM((STEPS, WIN * BW), F32),
            pltpu.VMEM((2 * BW, 2 * BW), BF16),
            pltpu.VMEM((NZ, 2 * NZ), BF16),
            field, field, field,
            pltpu.VMEM((STEPS + 1, WIN, NZ, BW), F32),
            parts, parts,
            pltpu.VMEM((WIN, 8, BW), F32),
            pltpu.VMEM((STEPS + 1, WIN, 8, BW), F32),
            pltpu.SMEM((NB,), jnp.int32),
            pltpu.SMEM((NB,), jnp.int32),
            pltpu.SMEM((1, WIN), jnp.int32),
            pltpu.SemaphoreType.DMA((9,)),
        ],
        compiler_params=pltpu.CompilerParams(vmem_limit_bytes=58 << 20),
        name="wave",
    )(
        source_cell, block_place, lit_blocks, courant_sq, start_field, adjoint_state, observed,
        jnp.asarray(lateral_matrix(), BF16), jnp.asarray(depth_matrix(), BF16),
    )
    from_second, from_third = shift(pieces[2], "y", N_Y, 2), shift(pieces[3], "y", N_Y, 3)
    near = jnp.concatenate([pieces[0], shift(pieces[1], "y", N_Y, 1)], 0)
    far = pl.pallas_call(
        stack_kernel,
        out_shape=jax.ShapeDtypeStruct((WIN // 2, NZ, BW), F32),
        in_specs=[pl.BlockSpec(memory_space=pl.ANY)] + [vmem] * 2,
        out_specs=vmem,
        compiler_params=pltpu.CompilerParams(vmem_limit_bytes=16 << 20),
        name="stack",
    )(near, from_second, from_third)
    near_left, near_right = shift(near, "x", N_X, 1), shift(near, "x", N_X, -1)
    far_left, far_right = shift(far, "x", N_X, 1), shift(far, "x", N_X, -1)
    gathered = (
        near, far, near_left, far_left, near_right, far_right,
        shift(near_left, "x", N_X, 1), shift(far_right, "x", N_X, -1),
    )
    other, own = (
        pl.pallas_call(
            functools.partial(route_kernel, lowest),
            out_shape=jax.ShapeDtypeStruct((N_Z, NZ, BW), F32),
            in_specs=[smem] + [vmem] * len(gathered),
            out_specs=vmem,
            compiler_params=pltpu.CompilerParams(vmem_limit_bytes=16 << 20),
            cost_estimate=pl.CostEstimate(flops=1 << 18, bytes_accessed=1 << 21, transcendentals=0),
            name=name,
        )(table, *gathered)
        for lowest, name in ((N_Z, "route_other"), (0, "route_own"))
    )
    here, up, down, up_three, down_three = pl.pallas_call(
        join_kernel,
        out_shape=tuple(jax.ShapeDtypeStruct((len(g), NZ, BW), F32) for g in Z_GROUPS),
        in_specs=[vmem, vmem],
        out_specs=(vmem,) * len(Z_GROUPS),
        compiler_params=pltpu.CompilerParams(vmem_limit_bytes=16 << 20),
        name="join",
    )(own, shift(other, "core", N_CORE, 1))
    up, down = shift(up, "z", N_Z, 1), shift(down, "z", N_Z, -1)
    up_three = shift(up_three + up[1:2] + down[1:], "z", N_Z, 3)
    down_three = shift(down_three + up[2:], "z", N_Z, -3)
    return (here + up[:1] + down[:1]) + (up_three + down_three)


def solution(mesh):
    split_mesh = Mesh(mesh.devices.reshape(N_Z, N_X, N_CORE, N_Y), AXES)
    split = P(AXES, None, None)
    return jax.shard_map(
        local,
        mesh=split_mesh,
        in_specs=(split, split, split, split, P(), P(AXES, None), P()),
        out_specs=split,
        check_vma=False,
    )
```
